32 devices in a mesh: res: 8 (over y, x, core), seq: 4 (over z).
Axes of the slice: x: 2, y: 2, z: 4, core: 2. Of those that a mesh axis runs over, the one named last changes fastest.
Arguments:
- alignment_input: bfloat16 [64, 64, 256], P('seq', 'res'), may hold values from -8 to 8
- pairwise_input: bfloat16 [64, 64, 128], P('res'), may hold values from -6 to 6
- pairwise_norm_gain: float32 [128], replicated, may hold values from 0.1 to 1.9
- pair_bias_matrix: bfloat16 [128, 8], replicated, may hold values from -0.5 to 0.5
- row_attention_norm_gain: float32 [256], replicated, may hold values from 0.1 to 1.9
- row_attention_query_weight: bfloat16 [256, 256], replicated, may hold values from -2 to 2
- row_attention_key_weight: bfloat16 [256, 256], replicated, may hold values from -2 to 2
- row_attention_value_weight: bfloat16 [256, 256], replicated, may hold values from -0.375 to 0.375
- row_attention_gate_weight: bfloat16 [256, 256], replicated, may hold values from -0.375 to 0.375
- row_attention_gate_bias: float32 [256], replicated, may hold values from -4 to 4
- row_output_weight: bfloat16 [256, 256], replicated, may hold values from -0.375 to 0.375
- row_output_bias: float32 [256], replicated, may hold values from -1.5 to 1.5
- column_attention_norm_gain: float32 [256], replicated, may hold values from 0.1 to 1.9
- column_attention_query_weight: bfloat16 [256, 256], replicated, may hold values from -2 to 2
- column_attention_key_weight: bfloat16 [256, 256], replicated, may hold values from -2 to 2
- column_attention_value_weight: bfloat16 [256, 256], replicated, may hold values from -0.375 to 0.375
- column_attention_gate_weight: bfloat16 [256, 256], replicated, may hold values from -0.375 to 0.375
- column_attention_gate_bias: float32 [256], replicated, may hold values from -4 to 4
- column_output_weight: bfloat16 [256, 256], replicated, may hold values from -0.375 to 0.375
- column_output_bias: float32 [256], replicated, may hold values from -1.5 to 1.5
- transition_norm_gain: float32 [256], replicated, may hold values from 0.1 to 1.9
- transition_input_weight: bfloat16 [256, 1024], replicated, may hold values from -0.375 to 0.375
- transition_input_bias: float32 [1024], replicated, may hold values from -2.5 to 2.5
- transition_output_weight: bfloat16 [1024, 256], replicated, may hold values from -0.1875 to 0.1875
- transition_output_bias: float32 [256], replicated, may hold values from -1.5 to 1.5
- outer_product_norm_gain: float32 [256], replicated, may hold values from 0.1 to 1.9
- left_projection_weight: bfloat16 [256, 32], replicated, may hold values from -0.375 to 0.375
- right_projection_weight: bfloat16 [256, 32], replicated, may hold values from -0.375 to 0.375
- outer_output_weight: float32 [1024, 128], replicated, may hold values from -3 to 3
- outer_output_bias: float32 [128], replicated, may hold values from -1.5 to 1.5
Outputs:
- alignment_output: bfloat16 [64, 64, 256], P('seq', 'res')
- pairwise_output: bfloat16 [64, 64, 128], P('res')
The draws below stay inside these ranges and needn't reach their ends.
All inputs are finite; a program needn't handle non-finite values.
Results may differ from the reference program's by a relative error of at most 0.015.
Values may be sent and summed in bfloat16 or wider, within the bound.
A program may use at most 128 MiB of HBM per device.

```python
import jax
import jax.numpy as jnp
from jax import lax

ALIGNMENT_WIDTH = 256
PAIR_CH = 128
HEADS = 8
HEAD_DIM = 32
FACTOR_WIDTH = 32
TRANSITION_UNITS = 1024
SEQUENCE_COUNT = 64
RESIDUE_COUNT = 64


def square_normal(key):
    return jnp.clip(jax.random.normal(key, (ALIGNMENT_WIDTH, ALIGNMENT_WIDTH), jnp.float32), -6.0, 6.0) * ALIGNMENT_WIDTH ** (-0.5)


def draw_alignment_input(key, part):
    key = jax.random.fold_in(key, 1)
    return jnp.clip(jax.random.normal(key, (SEQUENCE_COUNT, RESIDUE_COUNT, ALIGNMENT_WIDTH), jnp.float32), -8.0, 8.0).astype(jnp.bfloat16)


def draw_row_attention_query_weight(key, part):
    key = jax.random.fold_in(key, 3)
    return square_normal(key).astype(jnp.bfloat16)


def draw_row_attention_key_weight(key, part):
    key = jax.random.fold_in(key, 4)
    return square_normal(key).astype(jnp.bfloat16)


def draw_column_attention_query_weight(key, part):
    key = jax.random.fold_in(key, 5)
    return square_normal(key).astype(jnp.bfloat16)


def draw_column_attention_key_weight(key, part):
    key = jax.random.fold_in(key, 6)
    return square_normal(key).astype(jnp.bfloat16)


def block_levels(rng, dims, cuts, smallest, high):
    factor_of = 1.0
    for axis_at, parts in cuts:
        draws = jax.random.uniform(jax.random.fold_in(jax.random.fold_in(rng, 6), axis_at), (parts,), jnp.float32, smallest / len(cuts), high / len(cuts))
        factor_of = factor_of * jnp.repeat(jnp.exp(draws), dims[axis_at] // parts).reshape((-1,) + (1,) * (len(dims) - 1 - axis_at))
    return factor_of


def normal_values(stream_key, dims, width, limit, shards=(), kind=jnp.bfloat16):
    values = jax.random.normal(stream_key, dims, jnp.float32) * width
    if len(shards) > 0:
        values = block_levels(stream_key, dims, shards, -0.22, 0.18) * values
    return jnp.clip(values, min=-limit, max=limit).astype(kind)


def setup_inputs(seed: int = 0) -> dict:
    streams_of = jax.random.split(jax.random.key(seed), 31)
    alignment_input = draw_alignment_input(jax.random.fold_in(streams_of[30], 71), 0)
    pairwise_input = normal_values(streams_of[1], (RESIDUE_COUNT, RESIDUE_COUNT, PAIR_CH), 1.0, 6.0, ((0, 8),))
    pairwise_norm_gain = jnp.clip(1.0 + 0.18 * jax.random.normal(streams_of[2], (PAIR_CH,), jnp.float32), 0.1, 1.9)
    pair_bias_matrix = normal_values(streams_of[3], (PAIR_CH, HEADS), PAIR_CH ** -0.5, 0.5)
    row_attention_norm_gain = jnp.clip(1.0 + 0.18 * jax.random.normal(streams_of[4], (ALIGNMENT_WIDTH,), jnp.float32), 0.1, 1.9)
    row_attention_query_weight = draw_row_attention_query_weight(jax.random.fold_in(streams_of[30], 71), 0)
    row_attention_key_weight = draw_row_attention_key_weight(jax.random.fold_in(streams_of[30], 71), 0)
    row_attention_value_weight = normal_values(streams_of[7], (ALIGNMENT_WIDTH, ALIGNMENT_WIDTH), ALIGNMENT_WIDTH ** -0.5, 0.375)
    row_attention_gate_weight = normal_values(streams_of[8], (ALIGNMENT_WIDTH, ALIGNMENT_WIDTH), ALIGNMENT_WIDTH ** -0.5, 0.375)
    row_attention_gate_bias = normal_values(streams_of[9], (ALIGNMENT_WIDTH,), 1.0, 4.0, (), jnp.float32)
    row_output_weight = normal_values(streams_of[10], (ALIGNMENT_WIDTH, ALIGNMENT_WIDTH), ALIGNMENT_WIDTH ** -0.5, 0.375)
    row_output_bias = normal_values(streams_of[11], (ALIGNMENT_WIDTH,), 0.3, 1.5, (), jnp.float32)
    column_attention_norm_gain = jnp.clip(1.0 + 0.18 * jax.random.normal(streams_of[12], (ALIGNMENT_WIDTH,), jnp.float32), 0.1, 1.9)
    column_attention_query_weight = draw_column_attention_query_weight(jax.random.fold_in(streams_of[30], 71), 0)
    column_attention_key_weight = draw_column_attention_key_weight(jax.random.fold_in(streams_of[30], 71), 0)
    column_attention_value_weight = normal_values(streams_of[15], (ALIGNMENT_WIDTH, ALIGNMENT_WIDTH), ALIGNMENT_WIDTH ** -0.5, 0.375)
    column_attention_gate_weight = normal_values(streams_of[16], (ALIGNMENT_WIDTH, ALIGNMENT_WIDTH), ALIGNMENT_WIDTH ** -0.5, 0.375)
    column_attention_gate_bias = normal_values(streams_of[17], (ALIGNMENT_WIDTH,), 1.0, 4.0, (), jnp.float32)
    column_output_weight = normal_values(streams_of[18], (ALIGNMENT_WIDTH, ALIGNMENT_WIDTH), ALIGNMENT_WIDTH ** -0.5, 0.375)
    column_output_bias = normal_values(streams_of[19], (ALIGNMENT_WIDTH,), 0.3, 1.5, (), jnp.float32)
    transition_norm_gain = jnp.clip(1.0 + 0.18 * jax.random.normal(streams_of[20], (ALIGNMENT_WIDTH,), jnp.float32), 0.1, 1.9)
    transition_input_weight = normal_values(streams_of[21], (ALIGNMENT_WIDTH, TRANSITION_UNITS), ALIGNMENT_WIDTH ** -0.5, 0.375)
    transition_input_bias = normal_values(streams_of[22], (TRANSITION_UNITS,), 0.5, 2.5, (), jnp.float32)
    transition_output_weight = normal_values(streams_of[23], (TRANSITION_UNITS, ALIGNMENT_WIDTH), TRANSITION_UNITS ** -0.5, 0.1875)
    transition_output_bias = normal_values(streams_of[24], (ALIGNMENT_WIDTH,), 0.3, 1.5, (), jnp.float32)
    outer_product_norm_gain = jnp.clip(1.0 + 0.18 * jax.random.normal(streams_of[25], (ALIGNMENT_WIDTH,), jnp.float32), 0.1, 1.9)
    left_projection_weight = normal_values(streams_of[26], (ALIGNMENT_WIDTH, FACTOR_WIDTH), ALIGNMENT_WIDTH ** -0.5, 0.375)
    right_projection_weight = normal_values(streams_of[27], (ALIGNMENT_WIDTH, FACTOR_WIDTH), ALIGNMENT_WIDTH ** -0.5, 0.375)
    outer_output_weight = normal_values(streams_of[28], (FACTOR_WIDTH * FACTOR_WIDTH, PAIR_CH), 0.5, 3.0, (), jnp.float32)
    outer_output_bias = normal_values(streams_of[29], (PAIR_CH,), 0.3, 1.5, (), jnp.float32)
    return dict(alignment_input=alignment_input, pairwise_input=pairwise_input, pairwise_norm_gain=pairwise_norm_gain, pair_bias_matrix=pair_bias_matrix, row_attention_norm_gain=row_attention_norm_gain, row_attention_query_weight=row_attention_query_weight, row_attention_key_weight=row_attention_key_weight, row_attention_value_weight=row_attention_value_weight, row_attention_gate_weight=row_attention_gate_weight, row_attention_gate_bias=row_attention_gate_bias, row_output_weight=row_output_weight, row_output_bias=row_output_bias, column_attention_norm_gain=column_attention_norm_gain, column_attention_query_weight=column_attention_query_weight, column_attention_key_weight=column_attention_key_weight, column_attention_value_weight=column_attention_value_weight, column_attention_gate_weight=column_attention_gate_weight, column_attention_gate_bias=column_attention_gate_bias, column_output_weight=column_output_weight, column_output_bias=column_output_bias, transition_norm_gain=transition_norm_gain, transition_input_weight=transition_input_weight, transition_input_bias=transition_input_bias, transition_output_weight=transition_output_weight, transition_output_bias=transition_output_bias, outer_product_norm_gain=outer_product_norm_gain, left_projection_weight=left_projection_weight, right_projection_weight=right_projection_weight, outer_output_weight=outer_output_weight, outer_output_bias=outer_output_bias)


EPSILON = 1e-05

def normalize_layer(values, norm_gain):
    center = values - lax.optimization_barrier(jnp.mean(values, axis=-1, keepdims=True))
    spread = lax.optimization_barrier(jnp.mean(center * center, axis=-1, keepdims=True))
    return center * lax.rsqrt(spread + EPSILON) * norm_gain

def attend(query_rows, key_rows, pair_bias, weights):
    query_weight, key_weight, value_weight, gate_weight, gate_bias, out_weight, out_bias = weights
    query_count = query_rows.shape[0]
    key_count = key_rows.shape[0]
    query_heads = jnp.dot(query_rows, query_weight, preferred_element_type=jnp.float32).astype(jnp.bfloat16).reshape(query_count, HEADS, HEAD_DIM)
    key_heads = jnp.dot(key_rows, key_weight, preferred_element_type=jnp.float32).astype(jnp.bfloat16).reshape(key_count, HEADS, HEAD_DIM)
    value_heads = jnp.dot(key_rows, value_weight, preferred_element_type=jnp.float32).astype(jnp.bfloat16).reshape(key_count, HEADS, HEAD_DIM)
    scores = jnp.einsum('qhd,khd->hqk', query_heads.astype(jnp.float32), key_heads.astype(jnp.float32)) * HEAD_DIM ** (-0.5)
    if pair_bias is not None:
        scores = scores + pair_bias.astype(jnp.float32)
    soft_weights = jax.nn.softmax(scores, axis=-1).astype(jnp.bfloat16)
    attended = jnp.einsum('hqk,khd->qhd', soft_weights.astype(jnp.float32), value_heads.astype(jnp.float32)).reshape(query_count, HEADS * HEAD_DIM)
    gate_values = jax.nn.sigmoid(jnp.dot(query_rows, gate_weight, preferred_element_type=jnp.float32) + gate_bias)
    gated_rows = (gate_values * attended).astype(jnp.bfloat16)
    return (jnp.dot(gated_rows, out_weight, preferred_element_type=jnp.float32) + out_bias).astype(jnp.bfloat16)

def reference(alignment_input, pairwise_input, pairwise_norm_gain, pair_bias_matrix, row_attention_norm_gain, row_attention_query_weight, row_attention_key_weight, row_attention_value_weight, row_attention_gate_weight, row_attention_gate_bias, row_output_weight, row_output_bias, column_attention_norm_gain, column_attention_query_weight, column_attention_key_weight, column_attention_value_weight, column_attention_gate_weight, column_attention_gate_bias, column_output_weight, column_output_bias, transition_norm_gain, transition_input_weight, transition_input_bias, transition_output_weight, transition_output_bias, outer_product_norm_gain, left_projection_weight, right_projection_weight, outer_output_weight, outer_output_bias):
    pair_normed = normalize_layer(pairwise_input.astype(jnp.float32), pairwise_norm_gain).astype(jnp.bfloat16)
    pair_bias = jnp.einsum('ijz,zh->hij', pair_normed.astype(jnp.float32), pair_bias_matrix.astype(jnp.float32)).astype(jnp.bfloat16)
    row_weights = (row_attention_query_weight, row_attention_key_weight, row_attention_value_weight, row_attention_gate_weight, row_attention_gate_bias, row_output_weight, row_output_bias)
    column_weights = (column_attention_query_weight, column_attention_key_weight, column_attention_value_weight, column_attention_gate_weight, column_attention_gate_bias, column_output_weight, column_output_bias)
    row_normalized = normalize_layer(alignment_input.astype(jnp.float32), row_attention_norm_gain).astype(jnp.bfloat16)
    row_delta = lax.map(lambda single: attend(single, single, pair_bias, row_weights), row_normalized)
    alignment_after_rows = alignment_input.astype(jnp.float32) + row_delta.astype(jnp.float32)
    column_normalized = normalize_layer(alignment_after_rows, column_attention_norm_gain).astype(jnp.bfloat16)
    column_delta = lax.map(lambda single: attend(single, single, None, column_weights), jnp.swapaxes(column_normalized, 0, 1))
    alignment_after_columns = alignment_after_rows + jnp.swapaxes(column_delta, 0, 1).astype(jnp.float32)
    transition_normalized = normalize_layer(alignment_after_columns, transition_norm_gain).astype(jnp.bfloat16)
    transition_hidden = jax.nn.relu(jnp.dot(transition_normalized, transition_input_weight, preferred_element_type=jnp.float32) + transition_input_bias).astype(jnp.bfloat16)
    alignment_output = (alignment_after_columns + jnp.dot(transition_hidden, transition_output_weight, preferred_element_type=jnp.float32) + transition_output_bias).astype(jnp.bfloat16)
    outer_normalized = normalize_layer(alignment_output.astype(jnp.float32), outer_product_norm_gain).astype(jnp.bfloat16)
    left_factor = jnp.dot(outer_normalized, left_projection_weight, preferred_element_type=jnp.float32).astype(jnp.bfloat16)
    right_factor = jnp.dot(outer_normalized, right_projection_weight, preferred_element_type=jnp.float32).astype(jnp.bfloat16)
    right_float = right_factor.astype(jnp.float32)

    def outer_row(left_row):
        sums = jnp.einsum('sc,sje->jce', left_row.astype(jnp.float32), right_float).reshape(RESIDUE_COUNT, FACTOR_WIDTH * FACTOR_WIDTH) / SEQUENCE_COUNT
        return jnp.dot(sums, outer_output_weight, precision=lax.Precision.HIGHEST)
    pair_update = lax.map(outer_row, jnp.swapaxes(left_factor, 0, 1))
    pairwise_output = (pairwise_input.astype(jnp.float32) + pair_update + outer_output_bias).astype(jnp.bfloat16)
    return (alignment_output, pairwise_output)
```

```python
import functools

import jax
import jax.numpy as jnp
from jax import lax
from jax.experimental import pallas as pl
from jax.experimental.pallas import tpu as pltpu
from jax.sharding import PartitionSpec as P

PAIR_CH = 128
HEADS = 8
HEAD_DIM = 32
FACTOR_WIDTH = 32


EPSILON = 1e-05


def normalize_layer(values, norm_gain):
    center = values - jnp.mean(values, axis=-1, keepdims=True)
    spread = jnp.mean(center * center, axis=-1, keepdims=True)
    return center * lax.rsqrt(spread + EPSILON) * norm_gain


def attend(query_rows, key_rows, pair_bias, weights):
    query_weight, key_weight, value_weight, gate_weight, gate_bias, out_weight, out_bias = weights
    query_count = query_rows.shape[0]
    key_count = key_rows.shape[0]
    query_heads = (
        jnp.dot(query_rows, query_weight, preferred_element_type=jnp.float32)
        .astype(jnp.bfloat16)
        .reshape(query_count, HEADS, HEAD_DIM)
    )
    key_heads = (
        jnp.dot(key_rows, key_weight, preferred_element_type=jnp.float32)
        .astype(jnp.bfloat16)
        .reshape(key_count, HEADS, HEAD_DIM)
    )
    value_heads = (
        jnp.dot(key_rows, value_weight, preferred_element_type=jnp.float32)
        .astype(jnp.bfloat16)
        .reshape(key_count, HEADS, HEAD_DIM)
    )
    scores = jnp.einsum(
        "qhd,khd->hqk", query_heads, key_heads, preferred_element_type=jnp.float32
    ) * HEAD_DIM ** (-0.5)
    if pair_bias is not None:
        scores = scores + pair_bias.astype(jnp.float32)
    soft_weights = jax.nn.softmax(scores, axis=-1).astype(jnp.bfloat16)
    attended = jnp.einsum(
        "hqk,khd->qhd", soft_weights, value_heads, preferred_element_type=jnp.float32
    ).reshape(query_count, HEADS * HEAD_DIM)
    gate_values = jax.nn.sigmoid(
        jnp.dot(query_rows, gate_weight, preferred_element_type=jnp.float32) + gate_bias
    )
    gated_rows = (gate_values * attended).astype(jnp.bfloat16)
    return (jnp.dot(gated_rows, out_weight, preferred_element_type=jnp.float32) + out_bias).astype(
        jnp.bfloat16
    )


def spread_body(
    alignment_input,
    pairwise_input,
    pairwise_norm_gain,
    pair_bias_matrix,
    row_attention_norm_gain,
    row_attention_query_weight,
    row_attention_key_weight,
    row_attention_value_weight,
    row_attention_gate_weight,
    row_attention_gate_bias,
    row_output_weight,
    row_output_bias,
    column_attention_norm_gain,
    column_attention_query_weight,
    column_attention_key_weight,
    column_attention_value_weight,
    column_attention_gate_weight,
    column_attention_gate_bias,
    column_output_weight,
    column_output_bias,
    transition_norm_gain,
    transition_input_weight,
    transition_input_bias,
    transition_output_weight,
    transition_output_bias,
    outer_product_norm_gain,
    left_projection_weight,
    right_projection_weight,
    outer_output_weight,
    outer_output_bias,
):
    sequence_local = alignment_input.shape[0]
    residue_local = alignment_input.shape[1]
    res_devices = lax.axis_size("res")
    seq_devices = lax.axis_size("seq")
    residues = residue_local * res_devices
    total_seqs = sequence_local * seq_devices
    outer_width = FACTOR_WIDTH * FACTOR_WIDTH
    pair_normed = normalize_layer(pairwise_input.astype(jnp.float32), pairwise_norm_gain).astype(
        jnp.bfloat16
    )
    local_bias = jnp.einsum(
        "ijz,zh->hij", pair_normed, pair_bias_matrix, preferred_element_type=jnp.float32
    ).astype(jnp.bfloat16)
    pair_bias = lax.all_gather(local_bias, "res", axis=1, tiled=True)
    row_weights = (
        row_attention_query_weight,
        row_attention_key_weight,
        row_attention_value_weight,
        row_attention_gate_weight,
        row_attention_gate_bias,
        row_output_weight,
        row_output_bias,
    )
    column_weights = (
        column_attention_query_weight,
        column_attention_key_weight,
        column_attention_value_weight,
        column_attention_gate_weight,
        column_attention_gate_bias,
        column_output_weight,
        column_output_bias,
    )
    row_normalized = normalize_layer(
        alignment_input.astype(jnp.float32), row_attention_norm_gain
    ).astype(jnp.bfloat16)
    whole_rows = lax.all_to_all(row_normalized, "res", split_axis=0, concat_axis=1, tiled=True)
    row_result = jax.vmap(lambda single: attend(single, single, pair_bias, row_weights))(whole_rows)
    row_delta = lax.all_to_all(row_result, "res", split_axis=1, concat_axis=0, tiled=True)
    alignment_after_rows = alignment_input.astype(jnp.float32) + row_delta.astype(jnp.float32)
    column_normalized = normalize_layer(alignment_after_rows, column_attention_norm_gain).astype(
        jnp.bfloat16
    )
    column_attend = jax.vmap(
        lambda query_rows, key_rows: attend(query_rows, key_rows, None, column_weights),
        in_axes=(1, 1),
        out_axes=1,
    )
    all_sequences = lax.all_gather(column_normalized, "seq", axis=0, tiled=True)
    column_delta = column_attend(column_normalized, all_sequences)
    alignment_after_columns = alignment_after_rows + column_delta.astype(jnp.float32)
    transition_normalized = normalize_layer(alignment_after_columns, transition_norm_gain).astype(
        jnp.bfloat16
    )
    transition_hidden = jax.nn.relu(
        jnp.dot(transition_normalized, transition_input_weight, preferred_element_type=jnp.float32)
        + transition_input_bias
    ).astype(jnp.bfloat16)
    alignment_output = (
        alignment_after_columns
        + jnp.dot(transition_hidden, transition_output_weight, preferred_element_type=jnp.float32)
        + transition_output_bias
    ).astype(jnp.bfloat16)
    outer_normalized = normalize_layer(
        alignment_output.astype(jnp.float32), outer_product_norm_gain
    ).astype(jnp.bfloat16)
    left_factor = jnp.dot(
        outer_normalized, left_projection_weight, preferred_element_type=jnp.float32
    ).astype(jnp.bfloat16)
    right_factor = jnp.dot(
        outer_normalized, right_projection_weight, preferred_element_type=jnp.float32
    ).astype(jnp.bfloat16)
    right_all = lax.all_gather(right_factor, "res", axis=1, tiled=True)
    left_flat = left_factor.reshape(sequence_local, residue_local * FACTOR_WIDTH)
    share_rows = residues // seq_devices
    right_piece = right_all.reshape(
        sequence_local, share_rows * lax.axis_size("seq") * FACTOR_WIDTH
    )
    product = lax.dot_general(
        left_flat, right_piece, (((0,), (0,)), ((), ())), preferred_element_type=jnp.float32
    )
    product = product.reshape(
        residue_local, FACTOR_WIDTH, share_rows * lax.axis_size("seq"), FACTOR_WIDTH
    ).transpose(2, 0, 1, 3)
    summed = lax.psum_scatter(
        product.reshape(share_rows * lax.axis_size("seq"), residue_local, outer_width).astype(
            jnp.bfloat16
        ),
        "seq",
        scatter_dimension=0,
        tiled=True,
    ).astype(jnp.float32)
    projected = jnp.dot(
        (summed / total_seqs).reshape(share_rows * residue_local, outer_width),
        outer_output_weight,
        precision=lax.Precision.HIGHEST,
    )
    projected = projected.reshape(share_rows, residue_local, PAIR_CH)
    pair_update = lax.all_gather(projected.astype(jnp.bfloat16), "seq", axis=0, tiled=True).astype(
        projected.dtype
    )
    pair_update = jnp.swapaxes(pair_update, 0, 1)
    pairwise_output = (pairwise_input.astype(jnp.float32) + pair_update + outer_output_bias).astype(
        jnp.bfloat16
    )
    return (alignment_output, pairwise_output)


F32 = jnp.float32
BF16 = jnp.bfloat16
MESH = pl.DeviceIdType.MESH


def mm(a, b):
    return jnp.dot(a, b, preferred_element_type=F32)


def mm_nt(a, b):
    return lax.dot_general(a, b, (((1,), (1,)), ((), ())), preferred_element_type=F32)


def row(ref):
    return ref[...].reshape(1, -1)


def swap_matrix(major, minor):
    size = major * minor
    to = lax.broadcasted_iota(jnp.int32, (size, size), 0)
    at = lax.broadcasted_iota(jnp.int32, (size, size), 1)
    return jnp.where(at == (to % major) * minor + to // major, 1.0, 0.0).astype(BF16)


def head_mask(width):
    lane = lax.broadcasted_iota(jnp.int32, (HEADS, 1, width), 2)
    head = lax.broadcasted_iota(jnp.int32, (HEADS, 1, width), 0)
    return jnp.where(lane // HEAD_DIM == head, 1.0, 0.0)


def softmax_rows(scores):
    e = jnp.exp(scores - jnp.max(scores, axis=-1, keepdims=True))
    return (e * (1.0 / jnp.sum(e, axis=-1, keepdims=True))).astype(BF16)


def block_kernel(
    res_n,
    seq_n,
    msa_ref,
    pair_ref,
    pair_gain,
    bias_w,
    row_gain,
    rq,
    rk,
    rv,
    rg,
    rgb,
    ro,
    rob,
    col_gain,
    cq,
    ck,
    cv,
    cg,
    cgb,
    co,
    cob,
    tr_gain,
    ti,
    tib,
    to,
    tob,
    op_gain,
    wl,
    wr,
    ow,
    ob,
    msa_out,
    pair_out,
    rows_all,
    in_send,
    in_all,
    up_send,
    up_all,
    back_send,
    back_all,
    right_all,
    right_f32,
    pair_all,
    key_buf,
    val_buf,
    t_buf,
    rows_ss,
    rows_rs,
    in_ss,
    in_rs,
    up_ss,
    up_rs,
    back_ss,
    back_rs,
    rz_ss,
    rz_rs,
    rr_ss,
    rr_rs,
    pz_ss,
    pz_rs,
):
    me_r = lax.axis_index("res")
    me_z = lax.axis_index("seq")
    s_loc, i_loc, width = msa_ref.shape
    residues = pair_ref.shape[1]
    rows = s_loc * i_loc
    share = i_loc // seq_n
    seqs = s_loc * seq_n
    block = share * s_loc
    scale = HEAD_DIM ** (-0.5)

    def res_peer(d):
        return lax.rem(me_r + d, res_n)

    def seq_peer(d):
        return lax.rem(me_z + d, seq_n)

    def send_res(src, dst, ss, rs, d):
        return pltpu.make_async_remote_copy(
            src_ref=src, dst_ref=dst, send_sem=ss, recv_sem=rs,
            device_id=(res_peer(d), me_z), device_id_type=MESH,
        )

    def send_seq(src, dst, ss, rs, d):
        return pltpu.make_async_remote_copy(
            src_ref=src, dst_ref=dst, send_sem=ss, recv_sem=rs,
            device_id=(me_r, seq_peer(d)), device_id_type=MESH,
        )

    barrier = pltpu.get_barrier_semaphore()
    for d in range(1, res_n):
        pl.semaphore_signal(barrier, inc=1, device_id=(res_peer(d), me_z), device_id_type=MESH)
    for d in range(1, seq_n):
        pl.semaphore_signal(barrier, inc=1, device_id=(me_r, seq_peer(d)), device_id_type=MESH)

    pending = []
    msa = msa_ref[...].astype(F32).reshape(rows, width)
    normed = normalize_layer(msa, row(row_gain)).astype(BF16)
    rows_all[me_r] = normed
    to_cols = swap_matrix(s_loc, i_loc)
    in_send[...] = mm(to_cols, msa.astype(BF16)).astype(BF16)

    pl.semaphore_wait(barrier, res_n - 1 + seq_n - 1)
    row_sends = []
    for d in range(1, res_n):
        c = send_res(rows_all.at[me_r], rows_all.at[me_r], rows_ss.at[d], rows_rs.at[d], d)
        c.start()
        row_sends.append(c)
    in_sends = []
    for d in range(1, seq_n):
        start = pl.multiple_of(seq_peer(d) * block, block)
        c = send_seq(in_send.at[pl.ds(start, block)], in_all.at[me_z], in_ss.at[d], in_rs.at[d], d)
        c.start()
        in_sends.append(c)
    own = pl.multiple_of(me_z * block, block)
    in_all[me_z] = in_send[pl.ds(own, block)]

    pair_f32 = pair_ref[...].astype(F32).reshape(i_loc * residues, PAIR_CH)
    pair_normed = normalize_layer(pair_f32, row(pair_gain)).astype(BF16)
    bias_t = bias_w[...].astype(F32).T.astype(BF16)
    by_residue = [
        mm_nt(bias_t, pair_normed[i * residues : (i + 1) * residues]) for i in range(i_loc)
    ]
    by_residue = jnp.concatenate(by_residue, axis=0).astype(BF16)
    bias = mm(swap_matrix(i_loc, HEADS), by_residue)

    mask = head_mask(width)
    queries = mm(normed, rq[...])
    gate = jax.nn.sigmoid(mm(normed, rg[...]) + row(rgb))

    def keys_of(src, data):
        key_buf[src] = mm(data, rk[...]).reshape(s_loc, i_loc, width)
        val_buf[src] = mm(data, rv[...]).reshape(s_loc, i_loc, width)

    keys_of(me_r, normed)
    half = FACTOR_WIDTH // 2
    spread = [
        jnp.concatenate(
            [
                ow[pl.ds(e, FACTOR_WIDTH, stride=FACTOR_WIDTH), :]
                for e in (k, half + k)
            ],
            axis=1,
        ).astype(BF16)
        for k in range(half)
    ]
    for d in range(1, res_n):
        row_sends[d - 1].wait_recv()
        src = lax.rem(me_r - d + res_n, res_n)
        keys_of(src, rows_all[src])

    scores = []
    for s in range(s_loc):
        q = queries[s * i_loc : (s + 1) * i_loc]
        q = (q[None] * mask).reshape(HEADS * i_loc, width).astype(BF16)
        k = key_buf[:, s].reshape(residues, width).astype(BF16)
        scores.append(mm_nt(q, k) * scale + bias)
    probs = [softmax_rows(x) for x in scores]
    attended = []
    for s in range(s_loc):
        v = val_buf[:, s].reshape(residues, width).astype(BF16)
        o = mm(probs[s], v).reshape(HEADS, i_loc, width)
        attended.append(jnp.sum(o * mask, axis=0))
    attended = jnp.concatenate(attended, axis=0)
    update = (mm((gate * attended).astype(BF16), ro[...]) + row(rob)).astype(BF16)
    up_send[...] = mm(to_cols, update).astype(BF16)
    up_sends = []
    for d in range(1, seq_n):
        start = pl.multiple_of(seq_peer(d) * block, block)
        c = send_seq(up_send.at[pl.ds(start, block)], up_all.at[me_z], up_ss.at[d], up_rs.at[d], d)
        c.start()
        up_sends.append(c)
    up_all[me_z] = up_send[pl.ds(own, block)]
    for c in in_sends:
        c.wait_recv()
    for c in up_sends:
        c.wait_recv()

    both = in_all[...].astype(F32) + up_all[...].astype(F32)
    both = both.reshape(seq_n, share, s_loc, width)
    first = jnp.concatenate([both[:, a].reshape(seqs, width) for a in range(share)], axis=0)
    normed = normalize_layer(first, row(col_gain)).astype(BF16)
    queries = mm(normed, cq[...])
    keys = mm(normed, ck[...]).astype(BF16)
    values = mm(normed, cv[...]).astype(BF16)
    gate = jax.nn.sigmoid(mm(normed, cg[...]) + row(cgb))
    attended = []
    for a in range(share):
        at = slice(a * seqs, (a + 1) * seqs)
        q = (queries[at][None] * mask).reshape(HEADS * seqs, width).astype(BF16)
        p = softmax_rows(mm_nt(q, keys[at]) * scale)
        o = mm(p, values[at]).reshape(HEADS, seqs, width)
        attended.append(jnp.sum(o * mask, axis=0))
    attended = jnp.concatenate(attended, axis=0)
    update = (mm((gate * attended).astype(BF16), co[...]) + row(cob)).astype(BF16)
    second = first + update.astype(F32)
    normed = normalize_layer(second, row(tr_gain)).astype(BF16)
    hidden = jnp.maximum(mm(normed, ti[...]) + row(tib), 0.0).astype(BF16)
    final = (second + mm(hidden, to[...]) + row(tob)).astype(BF16)

    normed = normalize_layer(final.astype(F32), row(op_gain)).astype(BF16)
    right = mm(normed, wr[...]).T
    right = jnp.concatenate(
        [
            jnp.concatenate(
                [right[:half, a * seqs : (a + 1) * seqs], right[half:, a * seqs : (a + 1) * seqs]],
                axis=1,
            )
            for a in range(share)
        ],
        axis=0,
    )
    right_all[me_r, me_z] = right.astype(BF16)
    here = right_all.at[me_r, me_z]
    rz_sends = []
    for d in range(1, seq_n):
        c = send_seq(here, here, rz_ss.at[d], rz_rs.at[d], d)
        c.start()
        rz_sends.append(c)
    rr_sends = []
    for d in range(1, res_n):
        c = send_res(here, here, rr_ss.at[d, 0], rr_rs.at[d, 0], d)
        c.start()
        rr_sends.append(c)

    for t in range(seq_n):
        back_send[t] = jnp.concatenate(
            [final[a * seqs + t * s_loc : a * seqs + (t + 1) * s_loc] for a in range(share)],
            axis=0,
        )
    back_sends = []
    for d in range(1, seq_n):
        c = send_seq(
            back_send.at[seq_peer(d)], back_all.at[me_z], back_ss.at[d], back_rs.at[d], d
        )
        c.start()
        back_sends.append(c)
    back_all[me_z] = back_send[me_z]

    for k in range(1, seq_n):
        rz_sends[k - 1].wait_recv()
        there = right_all.at[me_r, lax.rem(me_z - k + seq_n, seq_n)]
        for d in range(1, res_n):
            c = send_res(there, there, rr_ss.at[d, k], rr_rs.at[d, k], d)
            c.start()
            rr_sends.append(c)

    left = mm(normed, wl[...]).astype(BF16)
    for k in range(half):
        t = mm(left, spread[k])
        for p in range(2):
            t_buf[pl.ds((2 * k + p) * seqs, seqs), :] = jnp.concatenate(
                [
                    t[a * seqs : (a + 1) * seqs, p * PAIR_CH : (p + 1) * PAIR_CH]
                    for a in range(share)
                ],
                axis=1,
            ).astype(BF16)

    for c in back_sends:
        c.wait_recv()
    from_cols = swap_matrix(i_loc, s_loc)
    back = mm(from_cols, back_all[...].reshape(rows, width))
    msa_out[...] = back.reshape(s_loc, i_loc, width).astype(BF16)

    for c in rr_sends:
        c.wait_recv()
    right_f32[...] = right_all[...].astype(F32).reshape(right_f32.shape)
    right_rows = jnp.concatenate(
        [right_f32[pl.ds(k, residues, stride=half), :].astype(BF16) for k in range(half)], axis=1
    )
    change = mm(right_rows, t_buf[...]) * (1.0 / seqs)
    pair_all[me_z] = jnp.concatenate(
        [change[:, a * PAIR_CH : (a + 1) * PAIR_CH] for a in range(share)], axis=0
    ).astype(BF16)
    here = pair_all.at[me_z]
    pz_sends = []
    for d in range(1, seq_n):
        c = send_seq(here, here, pz_ss.at[d], pz_rs.at[d], d)
        c.start()
        pz_sends.append(c)
    for c in row_sends + in_sends + up_sends + rz_sends + rr_sends + back_sends:
        c.wait_send()
    for c in pz_sends:
        c.wait_recv()
    change = pair_all[...].astype(F32).reshape(i_loc, residues, PAIR_CH)
    pair_out[...] = (pair_ref[...].astype(F32) + change + ob[...].reshape(1, 1, -1)).astype(BF16)
    for c in pz_sends:
        c.wait_send()


def kernel_body(res_n, seq_n, *args):
    msa, pair = args[:2]
    s_loc, i_loc, width = msa.shape
    residues = pair.shape[1]
    rows = s_loc * i_loc
    share = i_loc // seq_n
    seqs = s_loc * seq_n
    block = share * s_loc
    factor_rows = share * FACTOR_WIDTH // 2
    dma = pltpu.SemaphoreType.DMA
    scratch = [
        pltpu.VMEM((res_n, rows, width), BF16),
        pltpu.VMEM((rows, width), BF16),
        pltpu.VMEM((seq_n, block, width), BF16),
        pltpu.VMEM((rows, width), BF16),
        pltpu.VMEM((seq_n, block, width), BF16),
        pltpu.VMEM((seq_n, block, width), BF16),
        pltpu.VMEM((seq_n, block, width), BF16),
        pltpu.VMEM((res_n, seq_n, factor_rows, 2 * seqs), BF16),
        pltpu.VMEM((res_n * seq_n * factor_rows, 2 * seqs), F32),
        pltpu.VMEM((seq_n, share * residues, PAIR_CH), BF16),
        pltpu.VMEM((res_n, s_loc, i_loc, width), F32),
        pltpu.VMEM((res_n, s_loc, i_loc, width), F32),
        pltpu.VMEM((FACTOR_WIDTH * seqs, share * PAIR_CH), BF16),
    ]
    scratch += [dma((res_n,))] * 2 + [dma((seq_n,))] * 8
    scratch += [dma((res_n, seq_n))] * 2 + [dma((seq_n,))] * 2
    vmem = pl.BlockSpec(memory_space=pltpu.VMEM)
    return pl.pallas_call(
        functools.partial(block_kernel, res_n, seq_n),
        out_shape=(
            jax.ShapeDtypeStruct(msa.shape, BF16),
            jax.ShapeDtypeStruct(pair.shape, BF16),
        ),
        in_specs=[vmem] * len(args),
        out_specs=(vmem, vmem),
        scratch_shapes=scratch,
        compiler_params=pltpu.CompilerParams(
            collective_id=0, has_side_effects=True, vmem_limit_bytes=48 * 1024 * 1024
        ),
        name="msa_block",
    )(*args)


def body(*args):
    msa = args[0]
    res_n = lax.axis_size("res")
    seq_n = lax.axis_size("seq")
    share = msa.shape[1] // seq_n
    small = (
        msa.shape[0] == 16
        and msa.shape[1] == 8
        and share == 2
        and msa.shape[0] * seq_n == 64
        and res_n * msa.shape[1] == 64
    )
    if small:
        return kernel_body(res_n, seq_n, *args)
    return spread_body(*args)


def solution(mesh):
    return jax.shard_map(
        body,
        mesh=mesh,
        in_specs=(
            P("seq", "res", None),
            P("res", None, None),
            P(),
            P(),
            P(),
            P(),
            P(),
            P(),
            P(),
            P(),
            P(),
            P(),
            P(),
            P(),
            P(),
            P(),
            P(),
            P(),
            P(),
            P(),
            P(),
            P(),
            P(),
            P(),
            P(),
            P(),
            P(),
            P(),
            P(),
            P(),
        ),
        out_specs=(P("seq", "res", None), P("res", None, None)),
        check_vma=False,
    )
```

```python
import functools

import jax
import jax.numpy as jnp
from jax import lax
from jax.experimental import pallas as pl
from jax.experimental.pallas import tpu as pltpu
from jax.sharding import PartitionSpec as P

PAIR_CH = 128
HEADS = 8
HEAD_DIM = 32
FACTOR_WIDTH = 32


EPSILON = 1e-05


def normalize_layer(values, norm_gain):
    center = values - jnp.mean(values, axis=-1, keepdims=True)
    spread = jnp.mean(center * center, axis=-1, keepdims=True)
    return center * lax.rsqrt(spread + EPSILON) * norm_gain


def attend(query_rows, key_rows, pair_bias, weights):
    query_weight, key_weight, value_weight, gate_weight, gate_bias, out_weight, out_bias = weights
    query_count = query_rows.shape[0]
    key_count = key_rows.shape[0]
    query_heads = (
        jnp.dot(query_rows, query_weight, preferred_element_type=jnp.float32)
        .astype(jnp.bfloat16)
        .reshape(query_count, HEADS, HEAD_DIM)
    )
    key_heads = (
        jnp.dot(key_rows, key_weight, preferred_element_type=jnp.float32)
        .astype(jnp.bfloat16)
        .reshape(key_count, HEADS, HEAD_DIM)
    )
    value_heads = (
        jnp.dot(key_rows, value_weight, preferred_element_type=jnp.float32)
        .astype(jnp.bfloat16)
        .reshape(key_count, HEADS, HEAD_DIM)
    )
    scores = jnp.einsum(
        "qhd,khd->hqk", query_heads, key_heads, preferred_element_type=jnp.float32
    ) * HEAD_DIM ** (-0.5)
    if pair_bias is not None:
        scores = scores + pair_bias.astype(jnp.float32)
    soft_weights = jax.nn.softmax(scores, axis=-1).astype(jnp.bfloat16)
    attended = jnp.einsum(
        "hqk,khd->qhd", soft_weights, value_heads, preferred_element_type=jnp.float32
    ).reshape(query_count, HEADS * HEAD_DIM)
    gate_values = jax.nn.sigmoid(
        jnp.dot(query_rows, gate_weight, preferred_element_type=jnp.float32) + gate_bias
    )
    gated_rows = (gate_values * attended).astype(jnp.bfloat16)
    return (jnp.dot(gated_rows, out_weight, preferred_element_type=jnp.float32) + out_bias).astype(
        jnp.bfloat16
    )


def spread_body(
    alignment_input,
    pairwise_input,
    pairwise_norm_gain,
    pair_bias_matrix,
    row_attention_norm_gain,
    row_attention_query_weight,
    row_attention_key_weight,
    row_attention_value_weight,
    row_attention_gate_weight,
    row_attention_gate_bias,
    row_output_weight,
    row_output_bias,
    column_attention_norm_gain,
    column_attention_query_weight,
    column_attention_key_weight,
    column_attention_value_weight,
    column_attention_gate_weight,
    column_attention_gate_bias,
    column_output_weight,
    column_output_bias,
    transition_norm_gain,
    transition_input_weight,
    transition_input_bias,
    transition_output_weight,
    transition_output_bias,
    outer_product_norm_gain,
    left_projection_weight,
    right_projection_weight,
    outer_output_weight,
    outer_output_bias,
):
    sequence_local = alignment_input.shape[0]
    residue_local = alignment_input.shape[1]
    res_devices = lax.axis_size("res")
    seq_devices = lax.axis_size("seq")
    residues = residue_local * res_devices
    total_seqs = sequence_local * seq_devices
    outer_width = FACTOR_WIDTH * FACTOR_WIDTH
    pair_normed = normalize_layer(pairwise_input.astype(jnp.float32), pairwise_norm_gain).astype(
        jnp.bfloat16
    )
    local_bias = jnp.einsum(
        "ijz,zh->hij", pair_normed, pair_bias_matrix, preferred_element_type=jnp.float32
    ).astype(jnp.bfloat16)
    pair_bias = lax.all_gather(local_bias, "res", axis=1, tiled=True)
    row_weights = (
        row_attention_query_weight,
        row_attention_key_weight,
        row_attention_value_weight,
        row_attention_gate_weight,
        row_attention_gate_bias,
        row_output_weight,
        row_output_bias,
    )
    column_weights = (
        column_attention_query_weight,
        column_attention_key_weight,
        column_attention_value_weight,
        column_attention_gate_weight,
        column_attention_gate_bias,
        column_output_weight,
        column_output_bias,
    )
    row_normalized = normalize_layer(
        alignment_input.astype(jnp.float32), row_attention_norm_gain
    ).astype(jnp.bfloat16)
    whole_rows = lax.all_to_all(row_normalized, "res", split_axis=0, concat_axis=1, tiled=True)
    row_result = jax.vmap(lambda single: attend(single, single, pair_bias, row_weights))(whole_rows)
    row_delta = lax.all_to_all(row_result, "res", split_axis=1, concat_axis=0, tiled=True)
    alignment_after_rows = alignment_input.astype(jnp.float32) + row_delta.astype(jnp.float32)
    column_normalized = normalize_layer(alignment_after_rows, column_attention_norm_gain).astype(
        jnp.bfloat16
    )
    column_attend = jax.vmap(
        lambda query_rows, key_rows: attend(query_rows, key_rows, None, column_weights),
        in_axes=(1, 1),
        out_axes=1,
    )
    all_sequences = lax.all_gather(column_normalized, "seq", axis=0, tiled=True)
    column_delta = column_attend(column_normalized, all_sequences)
    alignment_after_columns = alignment_after_rows + column_delta.astype(jnp.float32)
    transition_normalized = normalize_layer(alignment_after_columns, transition_norm_gain).astype(
        jnp.bfloat16
    )
    transition_hidden = jax.nn.relu(
        jnp.dot(transition_normalized, transition_input_weight, preferred_element_type=jnp.float32)
        + transition_input_bias
    ).astype(jnp.bfloat16)
    alignment_output = (
        alignment_after_columns
        + jnp.dot(transition_hidden, transition_output_weight, preferred_element_type=jnp.float32)
        + transition_output_bias
    ).astype(jnp.bfloat16)
    outer_normalized = normalize_layer(
        alignment_output.astype(jnp.float32), outer_product_norm_gain
    ).astype(jnp.bfloat16)
    left_factor = jnp.dot(
        outer_normalized, left_projection_weight, preferred_element_type=jnp.float32
    ).astype(jnp.bfloat16)
    right_factor = jnp.dot(
        outer_normalized, right_projection_weight, preferred_element_type=jnp.float32
    ).astype(jnp.bfloat16)
    right_all = lax.all_gather(right_factor, "res", axis=1, tiled=True)
    left_flat = left_factor.reshape(sequence_local, residue_local * FACTOR_WIDTH)
    share_rows = residues // seq_devices
    right_piece = right_all.reshape(
        sequence_local, share_rows * lax.axis_size("seq") * FACTOR_WIDTH
    )
    product = lax.dot_general(
        left_flat, right_piece, (((0,), (0,)), ((), ())), preferred_element_type=jnp.float32
    )
    product = product.reshape(
        residue_local, FACTOR_WIDTH, share_rows * lax.axis_size("seq"), FACTOR_WIDTH
    ).transpose(2, 0, 1, 3)
    summed = lax.psum_scatter(
        product.reshape(share_rows * lax.axis_size("seq"), residue_local, outer_width).astype(
            jnp.bfloat16
        ),
        "seq",
        scatter_dimension=0,
        tiled=True,
    ).astype(jnp.float32)
    projected = jnp.dot(
        (summed / total_seqs).reshape(share_rows * residue_local, outer_width),
        outer_output_weight,
        precision=lax.Precision.HIGHEST,
    )
    projected = projected.reshape(share_rows, residue_local, PAIR_CH)
    pair_update = lax.all_gather(projected.astype(jnp.bfloat16), "seq", axis=0, tiled=True).astype(
        projected.dtype
    )
    pair_update = jnp.swapaxes(pair_update, 0, 1)
    pairwise_output = (pairwise_input.astype(jnp.float32) + pair_update + outer_output_bias).astype(
        jnp.bfloat16
    )
    return (alignment_output, pairwise_output)


F32 = jnp.float32
BF16 = jnp.bfloat16
MESH = pl.DeviceIdType.MESH


def mm(a, b):
    return jnp.dot(a, b, preferred_element_type=F32)


def mm_nt(a, b):
    return lax.dot_general(a, b, (((1,), (1,)), ((), ())), preferred_element_type=F32)


def row(ref):
    return ref[...].reshape(1, -1)


def swap_matrix(major, minor):
    size = major * minor
    to = lax.broadcasted_iota(jnp.int32, (size, size), 0)
    at = lax.broadcasted_iota(jnp.int32, (size, size), 1)
    return jnp.where(at == (to % major) * minor + to // major, 1.0, 0.0).astype(BF16)


def head_mask(width):
    lane = lax.broadcasted_iota(jnp.int32, (HEADS, 1, width), 2)
    head = lax.broadcasted_iota(jnp.int32, (HEADS, 1, width), 0)
    return jnp.where(lane // HEAD_DIM == head, 1.0, 0.0)


def softmax_rows(scores):
    e = jnp.exp(scores - jnp.max(scores, axis=-1, keepdims=True))
    return (e * (1.0 / jnp.sum(e, axis=-1, keepdims=True))).astype(BF16)


ARGS = (
    "msa",
    "pair",
    "pair_gain",
    "bias_w",
    "row_gain",
    "rq",
    "rk",
    "rv",
    "rg",
    "rgb",
    "ro",
    "rob",
    "col_gain",
    "cq",
    "ck",
    "cv",
    "cg",
    "cgb",
    "co",
    "cob",
    "tr_gain",
    "ti",
    "tib",
    "to",
    "tob",
    "op_gain",
    "wl",
    "wr",
    "ow",
    "ob",
)
LOAD_ORDER = (
    "msa",
    "row_gain",
    "pair",
    "pair_gain",
    "bias_w",
    "rk",
    "rv",
    "rq",
    "rg",
    "rgb",
    "ow",
    "ro",
    "rob",
    "col_gain",
    "cq",
    "ck",
    "cv",
    "cg",
    "cgb",
    "co",
    "cob",
    "tr_gain",
    "ti",
    "tib",
    "to",
    "tob",
    "op_gain",
    "wl",
    "wr",
    "ob",
)


class Loads:
    def __init__(self, sources, places, sems):
        self.copies = {}
        self.places = dict(zip(ARGS, places))
        self.ready = set()
        for k, name in enumerate(ARGS):
            self.copies[name] = pltpu.make_async_copy(sources[k], places[k], sems.at[k])

    def start(self, names):
        for name in names:
            self.copies[name].start()

    def __getitem__(self, name):
        if name not in self.ready:
            self.copies[name].wait()
            self.ready.add(name)
        return self.places[name]


def block_kernel(res_n, seq_n, *refs):
    count = len(ARGS)
    loads = Loads(refs[:count], refs[count + 2 : 2 * count + 2], refs[2 * count + 2])
    msa_out, pair_out = refs[count : count + 2]
    (
        rows_all,
        in_send,
        in_all,
        up_send,
        up_all,
        back_send,
        back_all,
        right_all,
        right_f32,
        left_all,
        msa_res,
        pair_res,
        key_buf,
        val_buf,
        t_buf,
        rows_ss,
        rows_rs,
        in_ss,
        in_rs,
        up_ss,
        up_rs,
        back_ss,
        back_rs,
        rz_ss,
        rz_rs,
        rr_ss,
        rr_rs,
        left_ss,
        left_rs,
        out_sems,
    ) = refs[2 * count + 3 :]
    loads.start(LOAD_ORDER[:2])
    me_r = lax.axis_index("res")
    me_z = lax.axis_index("seq")
    s_loc, i_loc, width = loads.places["msa"].shape
    residues = loads.places["pair"].shape[1]
    rows = s_loc * i_loc
    share = i_loc // seq_n
    seqs = s_loc * seq_n
    block = share * s_loc
    scale = HEAD_DIM ** (-0.5)

    chips = res_n // 2
    core = lax.rem(me_r, 2)
    sibling = me_r + 1 - 2 * core

    def chip_peer(d):
        return lax.rem(me_r + 2 * d, res_n)

    class ResGather:
        def __init__(self, buffer, ss, rs):
            self.buffer, self.ss, self.rs = buffer, ss, rs
            self.direct = {}
            self.passed = {}

        def copy(self, at, slot, peer):
            return send_res(self.buffer.at[at], self.ss.at[slot], self.rs.at[slot], peer)

        def start(self):
            for d in range(1, chips):
                self.direct[d] = self.copy(me_r, d, chip_peer(d))
                self.direct[d].start()
            self.passed[0] = self.copy(me_r, chips, sibling)
            self.passed[0].start()

        def arrive(self, d):
            self.direct[d].wait_recv()
            src = lax.rem(me_r - 2 * d + res_n, res_n)
            self.passed[d] = self.copy(src, chips + d, sibling)
            self.passed[d].start()
            return src

        def arrive_passed(self, d):
            self.passed[d].wait_recv()
            return lax.rem(sibling - 2 * d + res_n, res_n)

        def finish(self):
            for c in list(self.direct.values()) + list(self.passed.values()):
                c.wait_send()

    def seq_peer(d):
        return lax.rem(me_z + d, seq_n)

    def send_res(ref, ss, rs, peer):
        return pltpu.make_async_remote_copy(
            src_ref=ref, dst_ref=ref, send_sem=ss, recv_sem=rs,
            device_id=(peer, me_z), device_id_type=MESH,
        )

    def send_seq(src, dst, ss, rs, d):
        return pltpu.make_async_remote_copy(
            src_ref=src, dst_ref=dst, send_sem=ss, recv_sem=rs,
            device_id=(me_r, seq_peer(d)), device_id_type=MESH,
        )

    barrier = pltpu.get_barrier_semaphore()
    for peer in [chip_peer(d) for d in range(1, chips)] + [sibling]:
        pl.semaphore_signal(barrier, inc=1, device_id=(peer, me_z), device_id_type=MESH)
    for d in range(1, seq_n):
        pl.semaphore_signal(barrier, inc=1, device_id=(me_r, seq_peer(d)), device_id_type=MESH)

    loads.start(LOAD_ORDER[2:])
    msa = loads["msa"][...].astype(F32).reshape(rows, width)
    normed = normalize_layer(msa, row(loads["row_gain"])).astype(BF16)
    rows_all[me_r] = normed
    to_cols = swap_matrix(s_loc, i_loc)
    in_send[...] = mm(to_cols, msa.astype(BF16)).astype(BF16)

    pl.semaphore_wait(barrier, chips + seq_n - 1)
    row_gather = ResGather(rows_all, rows_ss, rows_rs)
    row_gather.start()
    in_sends = []
    for d in range(1, seq_n):
        start = pl.multiple_of(seq_peer(d) * block, block)
        c = send_seq(in_send.at[pl.ds(start, block)], in_all.at[me_z], in_ss.at[d], in_rs.at[d], d)
        c.start()
        in_sends.append(c)
    own = pl.multiple_of(me_z * block, block)
    in_all[me_z] = in_send[pl.ds(own, block)]

    pair_f32 = loads["pair"][...].astype(F32).reshape(i_loc * residues, PAIR_CH)
    pair_normed = normalize_layer(pair_f32, row(loads["pair_gain"])).astype(BF16)
    bias_t = loads["bias_w"][...]
    by_residue = [
        mm_nt(bias_t, pair_normed[i * residues : (i + 1) * residues]) for i in range(i_loc)
    ]
    by_residue = jnp.concatenate(by_residue, axis=0).astype(BF16)
    bias = mm(swap_matrix(i_loc, HEADS), by_residue)

    mask = head_mask(width)
    queries = mm(normed, loads["rq"][...])
    gate = jax.nn.sigmoid(mm(normed, loads["rg"][...]) + row(loads["rgb"]))

    def keys_of(src, data):
        key_buf[src] = mm(data, loads["rk"][...]).reshape(s_loc, i_loc, width)
        val_buf[src] = mm(data, loads["rv"][...]).reshape(s_loc, i_loc, width)

    keys_of(me_r, normed)
    half = FACTOR_WIDTH // 2
    spread = [
        jnp.concatenate(
            [
                loads["ow"][pl.ds(e, FACTOR_WIDTH, stride=FACTOR_WIDTH), :]
                for e in (k, half + k)
            ],
            axis=1,
        ).astype(BF16)
        for k in range(half)
    ]
    src = row_gather.arrive_passed(0)
    keys_of(src, rows_all[src])
    for d in range(1, chips):
        src = row_gather.arrive(d)
        keys_of(src, rows_all[src])
    for d in range(1, chips):
        src = row_gather.arrive_passed(d)
        keys_of(src, rows_all[src])

    scores = []
    for s in range(s_loc):
        q = queries[s * i_loc : (s + 1) * i_loc]
        q = (q[None] * mask).reshape(HEADS * i_loc, width).astype(BF16)
        k = key_buf[:, s].reshape(residues, width).astype(BF16)
        scores.append(mm_nt(q, k) * scale + bias)
    probs = [softmax_rows(x) for x in scores]
    attended = []
    for s in range(s_loc):
        v = val_buf[:, s].reshape(residues, width).astype(BF16)
        o = mm(probs[s], v).reshape(HEADS, i_loc, width)
        attended.append(jnp.sum(o * mask, axis=0))
    attended = jnp.concatenate(attended, axis=0)
    update = (mm((gate * attended).astype(BF16), loads["ro"][...]) + row(loads["rob"])).astype(BF16)
    up_send[...] = mm(to_cols, update).astype(BF16)
    up_sends = []
    for d in range(1, seq_n):
        start = pl.multiple_of(seq_peer(d) * block, block)
        c = send_seq(up_send.at[pl.ds(start, block)], up_all.at[me_z], up_ss.at[d], up_rs.at[d], d)
        c.start()
        up_sends.append(c)
    up_all[me_z] = up_send[pl.ds(own, block)]
    for c in in_sends:
        c.wait_recv()
    for c in up_sends:
        c.wait_recv()

    both = in_all[...].astype(F32) + up_all[...].astype(F32)
    both = both.reshape(seq_n, share, s_loc, width)
    first = jnp.concatenate([both[:, a].reshape(seqs, width) for a in range(share)], axis=0)
    normed = normalize_layer(first, row(loads["col_gain"])).astype(BF16)
    queries = mm(normed, loads["cq"][...])
    keys = mm(normed, loads["ck"][...]).astype(BF16)
    values = mm(normed, loads["cv"][...]).astype(BF16)
    gate = jax.nn.sigmoid(mm(normed, loads["cg"][...]) + row(loads["cgb"]))
    attended = []
    for a in range(share):
        at = slice(a * seqs, (a + 1) * seqs)
        q = (queries[at][None] * mask).reshape(HEADS * seqs, width).astype(BF16)
        p = softmax_rows(mm_nt(q, keys[at]) * scale)
        o = mm(p, values[at]).reshape(HEADS, seqs, width)
        attended.append(jnp.sum(o * mask, axis=0))
    attended = jnp.concatenate(attended, axis=0)
    update = (mm((gate * attended).astype(BF16), loads["co"][...]) + row(loads["cob"])).astype(BF16)
    second = first + update.astype(F32)
    normed = normalize_layer(second, row(loads["tr_gain"])).astype(BF16)
    hidden = jnp.maximum(mm(normed, loads["ti"][...]) + row(loads["tib"]), 0.0).astype(BF16)
    final = (second + mm(hidden, loads["to"][...]) + row(loads["tob"])).astype(BF16)

    normed = normalize_layer(final.astype(F32), row(loads["op_gain"])).astype(BF16)
    right = mm_nt(loads["wr"][...], normed)
    right = jnp.concatenate(
        [
            jnp.concatenate(
                [right[:half, a * seqs : (a + 1) * seqs], right[half:, a * seqs : (a + 1) * seqs]],
                axis=1,
            )
            for a in range(share)
        ],
        axis=0,
    )
    right_all[me_r, me_z] = right.astype(BF16)
    here = right_all.at[me_r, me_z]
    rz_sends = []
    for d in range(1, seq_n):
        c = send_seq(here, here, rz_ss.at[d], rz_rs.at[d], d)
        c.start()
        rz_sends.append(c)
    left_all[me_z] = mm_nt(loads["wl"][...], normed).astype(BF16)
    here = left_all.at[me_z]
    left_sends = []
    for d in range(1, seq_n):
        c = send_seq(here, here, left_ss.at[d], left_rs.at[d], d)
        c.start()
        left_sends.append(c)

    for t in range(seq_n):
        back_send[t] = jnp.concatenate(
            [final[a * seqs + t * s_loc : a * seqs + (t + 1) * s_loc] for a in range(share)],
            axis=0,
        )
    back_sends = []
    for d in range(1, seq_n):
        c = send_seq(
            back_send.at[seq_peer(d)], back_all.at[me_z], back_ss.at[d], back_rs.at[d], d
        )
        c.start()
        back_sends.append(c)
    back_all[me_z] = back_send[me_z]

    for c in rz_sends:
        c.wait_recv()
    right_gather = ResGather(right_all, rr_ss, rr_rs)
    right_gather.start()

    def left_term(t):
        left = left_all[t].astype(F32).T.astype(BF16)
        for k in range(half):
            term = mm(left, spread[k])
            for p in range(2):
                t_buf[t, pl.ds((2 * k + p) * seqs, seqs), :] = jnp.concatenate(
                    [
                        term[a * seqs : (a + 1) * seqs, p * PAIR_CH : (p + 1) * PAIR_CH]
                        for a in range(share)
                    ],
                    axis=1,
                ).astype(BF16)

    left_term(me_z)
    for k in range(1, seq_n):
        left_sends[k - 1].wait_recv()
        left_term(lax.rem(me_z - k + seq_n, seq_n))
        if k == 1:
            for d in range(1, chips):
                right_gather.arrive(d)

    for c in back_sends:
        c.wait_recv()
    from_cols = swap_matrix(i_loc, s_loc)
    back = mm(from_cols, back_all[...].reshape(rows, width))
    msa_res[...] = back.reshape(s_loc, i_loc, width).astype(BF16)
    msa_copy = pltpu.make_async_copy(msa_res, msa_out, out_sems.at[0])
    msa_copy.start()

    for d in range(chips):
        right_gather.arrive_passed(d)
    right_f32[...] = right_all[...].astype(F32).reshape(right_f32.shape)
    right_rows = jnp.concatenate(
        [right_f32[pl.ds(k, residues, stride=half), :].astype(BF16) for k in range(half)], axis=1
    )
    bias_out = row(loads["ob"])
    for t in range(seq_n):
        change = mm(right_rows, t_buf[t]) * (1.0 / seqs)
        for a in range(share):
            old = loads["pair"][t * share + a].astype(F32)
            new = old + change[:, a * PAIR_CH : (a + 1) * PAIR_CH] + bias_out
            pair_res[t * share + a] = new.astype(BF16)
    pair_copy = pltpu.make_async_copy(pair_res, pair_out, out_sems.at[1])
    pair_copy.start()
    for c in in_sends + up_sends + rz_sends + left_sends + back_sends:
        c.wait_send()
    row_gather.finish()
    right_gather.finish()
    msa_copy.wait()
    pair_copy.wait()


def copy_kernel(msa_in, pair_in, msa_out, pair_out, sems):
    copies = [
        pltpu.make_async_copy(msa_in, msa_out, sems.at[0]),
        pltpu.make_async_copy(pair_in, pair_out, sems.at[1]),
    ]
    for c in copies:
        c.start()
    for c in copies:
        c.wait()


def kernel_body(res_n, seq_n, *args):
    args = [a.T if name in ("bias_w", "wl", "wr") else a for name, a in zip(ARGS, args)]
    msa, pair = args[:2]
    s_loc, i_loc, width = msa.shape
    residues = pair.shape[1]
    rows = s_loc * i_loc
    share = i_loc // seq_n
    seqs = s_loc * seq_n
    block = share * s_loc
    factor_rows = share * FACTOR_WIDTH // 2
    dma = pltpu.SemaphoreType.DMA
    scratch = [pltpu.VMEM(a.shape, a.dtype) for a in args] + [dma((len(args),))]
    scratch += [
        pltpu.VMEM((res_n, rows, width), BF16),
        pltpu.VMEM((rows, width), BF16),
        pltpu.VMEM((seq_n, block, width), BF16),
        pltpu.VMEM((rows, width), BF16),
        pltpu.VMEM((seq_n, block, width), BF16),
        pltpu.VMEM((seq_n, block, width), BF16),
        pltpu.VMEM((seq_n, block, width), BF16),
        pltpu.VMEM((res_n, seq_n, factor_rows, 2 * seqs), BF16),
        pltpu.VMEM((res_n * seq_n * factor_rows, 2 * seqs), F32),
        pltpu.VMEM((seq_n, FACTOR_WIDTH, rows), BF16),
        pltpu.VMEM(msa.shape, BF16),
        pltpu.VMEM(pair.shape, BF16),
        pltpu.VMEM((res_n, s_loc, i_loc, width), F32),
        pltpu.VMEM((res_n, s_loc, i_loc, width), F32),
        pltpu.VMEM((seq_n, FACTOR_WIDTH * seqs, share * PAIR_CH), BF16),
    ]
    scratch += [dma((res_n,))] * 2 + [dma((seq_n,))] * 8
    scratch += [dma((res_n,))] * 2 + [dma((seq_n,))] * 2 + [dma((2,))]
    hbm = pl.BlockSpec(memory_space=pltpu.HBM)
    shapes = (
        jax.ShapeDtypeStruct(msa.shape, BF16),
        jax.ShapeDtypeStruct(pair.shape, BF16),
    )
    results = pl.pallas_call(
        functools.partial(block_kernel, res_n, seq_n),
        out_shape=shapes,
        in_specs=[hbm] * len(args),
        out_specs=(hbm, hbm),
        scratch_shapes=scratch,
        compiler_params=pltpu.CompilerParams(
            collective_id=0, has_side_effects=True, vmem_limit_bytes=64 * 1024 * 1024
        ),
        name="msa_block",
    )(*args)
    return pl.pallas_call(
        copy_kernel,
        out_shape=shapes,
        in_specs=[hbm] * 2,
        out_specs=(hbm, hbm),
        scratch_shapes=[dma((2,))],
        compiler_params=pltpu.CompilerParams(vmem_limit_bytes=64 * 1024 * 1024),
        name="results",
    )(*results)


def body(*args):
    msa = args[0]
    res_n = lax.axis_size("res")
    seq_n = lax.axis_size("seq")
    share = msa.shape[1] // seq_n
    small = (
        msa.shape[0] == 16
        and msa.shape[1] == 8
        and share == 2
        and msa.shape[0] * seq_n == 64
        and res_n * msa.shape[1] == 64
    )
    if small:
        return kernel_body(res_n, seq_n, *args)
    return spread_body(*args)


def solution(mesh):
    return jax.shard_map(
        body,
        mesh=mesh,
        in_specs=(
            P("seq", "res", None),
            P("res", None, None),
            P(),
            P(),
            P(),
            P(),
            P(),
            P(),
            P(),
            P(),
            P(),
            P(),
            P(),
            P(),
            P(),
            P(),
            P(),
            P(),
            P(),
            P(),
            P(),
            P(),
            P(),
            P(),
            P(),
            P(),
            P(),
            P(),
            P(),
            P(),
        ),
        out_specs=(P("seq", "res", None), P("res", None, None)),
        check_vma=False,
    )
```

```python
import functools

import jax
import jax.numpy as jnp
from jax import lax
from jax.experimental import pallas as pl
from jax.experimental.pallas import tpu as pltpu
from jax.sharding import PartitionSpec as P

PAIR_CH = 128
HEADS = 8
HEAD_DIM = 32
FACTOR_WIDTH = 32


EPSILON = 1e-05


def normalize_layer(values, norm_gain):
    center = values - jnp.mean(values, axis=-1, keepdims=True)
    spread = jnp.mean(center * center, axis=-1, keepdims=True)
    return center * lax.rsqrt(spread + EPSILON) * norm_gain


def attend(query_rows, key_rows, pair_bias, weights):
    query_weight, key_weight, value_weight, gate_weight, gate_bias, out_weight, out_bias = weights
    query_count = query_rows.shape[0]
    key_count = key_rows.shape[0]
    query_heads = (
        jnp.dot(query_rows, query_weight, preferred_element_type=jnp.float32)
        .astype(jnp.bfloat16)
        .reshape(query_count, HEADS, HEAD_DIM)
    )
    key_heads = (
        jnp.dot(key_rows, key_weight, preferred_element_type=jnp.float32)
        .astype(jnp.bfloat16)
        .reshape(key_count, HEADS, HEAD_DIM)
    )
    value_heads = (
        jnp.dot(key_rows, value_weight, preferred_element_type=jnp.float32)
        .astype(jnp.bfloat16)
        .reshape(key_count, HEADS, HEAD_DIM)
    )
    scores = jnp.einsum(
        "qhd,khd->hqk", query_heads, key_heads, preferred_element_type=jnp.float32
    ) * HEAD_DIM ** (-0.5)
    if pair_bias is not None:
        scores = scores + pair_bias.astype(jnp.float32)
    soft_weights = jax.nn.softmax(scores, axis=-1).astype(jnp.bfloat16)
    attended = jnp.einsum(
        "hqk,khd->qhd", soft_weights, value_heads, preferred_element_type=jnp.float32
    ).reshape(query_count, HEADS * HEAD_DIM)
    gate_values = jax.nn.sigmoid(
        jnp.dot(query_rows, gate_weight, preferred_element_type=jnp.float32) + gate_bias
    )
    gated_rows = (gate_values * attended).astype(jnp.bfloat16)
    return (jnp.dot(gated_rows, out_weight, preferred_element_type=jnp.float32) + out_bias).astype(
        jnp.bfloat16
    )


def spread_body(
    alignment_input,
    pairwise_input,
    pairwise_norm_gain,
    pair_bias_matrix,
    row_attention_norm_gain,
    row_attention_query_weight,
    row_attention_key_weight,
    row_attention_value_weight,
    row_attention_gate_weight,
    row_attention_gate_bias,
    row_output_weight,
    row_output_bias,
    column_attention_norm_gain,
    column_attention_query_weight,
    column_attention_key_weight,
    column_attention_value_weight,
    column_attention_gate_weight,
    column_attention_gate_bias,
    column_output_weight,
    column_output_bias,
    transition_norm_gain,
    transition_input_weight,
    transition_input_bias,
    transition_output_weight,
    transition_output_bias,
    outer_product_norm_gain,
    left_projection_weight,
    right_projection_weight,
    outer_output_weight,
    outer_output_bias,
):
    sequence_local = alignment_input.shape[0]
    residue_local = alignment_input.shape[1]
    res_devices = lax.axis_size("res")
    seq_devices = lax.axis_size("seq")
    residues = residue_local * res_devices
    total_seqs = sequence_local * seq_devices
    outer_width = FACTOR_WIDTH * FACTOR_WIDTH
    pair_normed = normalize_layer(pairwise_input.astype(jnp.float32), pairwise_norm_gain).astype(
        jnp.bfloat16
    )
    local_bias = jnp.einsum(
        "ijz,zh->hij", pair_normed, pair_bias_matrix, preferred_element_type=jnp.float32
    ).astype(jnp.bfloat16)
    pair_bias = lax.all_gather(local_bias, "res", axis=1, tiled=True)
    row_weights = (
        row_attention_query_weight,
        row_attention_key_weight,
        row_attention_value_weight,
        row_attention_gate_weight,
        row_attention_gate_bias,
        row_output_weight,
        row_output_bias,
    )
    column_weights = (
        column_attention_query_weight,
        column_attention_key_weight,
        column_attention_value_weight,
        column_attention_gate_weight,
        column_attention_gate_bias,
        column_output_weight,
        column_output_bias,
    )
    row_normalized = normalize_layer(
        alignment_input.astype(jnp.float32), row_attention_norm_gain
    ).astype(jnp.bfloat16)
    whole_rows = lax.all_to_all(row_normalized, "res", split_axis=0, concat_axis=1, tiled=True)
    row_result = jax.vmap(lambda single: attend(single, single, pair_bias, row_weights))(whole_rows)
    row_delta = lax.all_to_all(row_result, "res", split_axis=1, concat_axis=0, tiled=True)
    alignment_after_rows = alignment_input.astype(jnp.float32) + row_delta.astype(jnp.float32)
    column_normalized = normalize_layer(alignment_after_rows, column_attention_norm_gain).astype(
        jnp.bfloat16
    )
    column_attend = jax.vmap(
        lambda query_rows, key_rows: attend(query_rows, key_rows, None, column_weights),
        in_axes=(1, 1),
        out_axes=1,
    )
    all_sequences = lax.all_gather(column_normalized, "seq", axis=0, tiled=True)
    column_delta = column_attend(column_normalized, all_sequences)
    alignment_after_columns = alignment_after_rows + column_delta.astype(jnp.float32)
    transition_normalized = normalize_layer(alignment_after_columns, transition_norm_gain).astype(
        jnp.bfloat16
    )
    transition_hidden = jax.nn.relu(
        jnp.dot(transition_normalized, transition_input_weight, preferred_element_type=jnp.float32)
        + transition_input_bias
    ).astype(jnp.bfloat16)
    alignment_output = (
        alignment_after_columns
        + jnp.dot(transition_hidden, transition_output_weight, preferred_element_type=jnp.float32)
        + transition_output_bias
    ).astype(jnp.bfloat16)
    outer_normalized = normalize_layer(
        alignment_output.astype(jnp.float32), outer_product_norm_gain
    ).astype(jnp.bfloat16)
    left_factor = jnp.dot(
        outer_normalized, left_projection_weight, preferred_element_type=jnp.float32
    ).astype(jnp.bfloat16)
    right_factor = jnp.dot(
        outer_normalized, right_projection_weight, preferred_element_type=jnp.float32
    ).astype(jnp.bfloat16)
    right_all = lax.all_gather(right_factor, "res", axis=1, tiled=True)
    left_flat = left_factor.reshape(sequence_local, residue_local * FACTOR_WIDTH)
    share_rows = residues // seq_devices
    right_piece = right_all.reshape(
        sequence_local, share_rows * lax.axis_size("seq") * FACTOR_WIDTH
    )
    product = lax.dot_general(
        left_flat, right_piece, (((0,), (0,)), ((), ())), preferred_element_type=jnp.float32
    )
    product = product.reshape(
        residue_local, FACTOR_WIDTH, share_rows * lax.axis_size("seq"), FACTOR_WIDTH
    ).transpose(2, 0, 1, 3)
    summed = lax.psum_scatter(
        product.reshape(share_rows * lax.axis_size("seq"), residue_local, outer_width).astype(
            jnp.bfloat16
        ),
        "seq",
        scatter_dimension=0,
        tiled=True,
    ).astype(jnp.float32)
    projected = jnp.dot(
        (summed / total_seqs).reshape(share_rows * residue_local, outer_width),
        outer_output_weight,
        precision=lax.Precision.HIGHEST,
    )
    projected = projected.reshape(share_rows, residue_local, PAIR_CH)
    pair_update = lax.all_gather(projected.astype(jnp.bfloat16), "seq", axis=0, tiled=True).astype(
        projected.dtype
    )
    pair_update = jnp.swapaxes(pair_update, 0, 1)
    pairwise_output = (pairwise_input.astype(jnp.float32) + pair_update + outer_output_bias).astype(
        jnp.bfloat16
    )
    return (alignment_output, pairwise_output)


F32 = jnp.float32
BF16 = jnp.bfloat16
MESH = pl.DeviceIdType.MESH


def mm(a, b):
    return jnp.dot(a, b, preferred_element_type=F32)


def mm_nt(a, b):
    return lax.dot_general(a, b, (((1,), (1,)), ((), ())), preferred_element_type=F32)


def row(ref):
    return ref[...].reshape(1, -1)


def swap_matrix(major, minor):
    size = major * minor
    to = lax.broadcasted_iota(jnp.int32, (size, size), 0)
    at = lax.broadcasted_iota(jnp.int32, (size, size), 1)
    return jnp.where(at == (to % major) * minor + to // major, 1.0, 0.0).astype(BF16)


def head_mask(width):
    lane = lax.broadcasted_iota(jnp.int32, (HEADS, 1, width), 2)
    head = lax.broadcasted_iota(jnp.int32, (HEADS, 1, width), 0)
    return jnp.where(lane // HEAD_DIM == head, 1.0, 0.0)


def softmax_rows(scores):
    e = jnp.exp(scores - jnp.max(scores, axis=-1, keepdims=True))
    return (e * (1.0 / jnp.sum(e, axis=-1, keepdims=True))).astype(BF16)


ARGS = (
    "msa",
    "pair",
    "pair_gain",
    "bias_w",
    "row_gain",
    "rq",
    "rk",
    "rv",
    "rg",
    "rgb",
    "ro",
    "rob",
    "col_gain",
    "cq",
    "ck",
    "cv",
    "cg",
    "cgb",
    "co",
    "cob",
    "tr_gain",
    "ti",
    "tib",
    "to",
    "tob",
    "op_gain",
    "wl",
    "wr",
    "ow",
    "ob",
)
LOAD_ORDER = (
    "msa",
    "row_gain",
    "pair",
    "pair_gain",
    "bias_w",
    "rk",
    "rv",
    "rq",
    "rg",
    "rgb",
    "ow",
    "ro",
    "rob",
    "col_gain",
    "cq",
    "ck",
    "cv",
    "cg",
    "cgb",
    "co",
    "cob",
    "tr_gain",
    "ti",
    "tib",
    "to",
    "tob",
    "op_gain",
    "wl",
    "wr",
    "ob",
)


class Loads:
    def __init__(self, sources, places, sems):
        self.copies = {}
        self.places = dict(zip(ARGS, places))
        self.ready = set()
        for k, name in enumerate(ARGS):
            self.copies[name] = pltpu.make_async_copy(sources[k], places[k], sems.at[k])

    def start(self, names):
        for name in names:
            self.copies[name].start()

    def __getitem__(self, name):
        if name not in self.ready:
            self.copies[name].wait()
            self.ready.add(name)
        return self.places[name]


def block_kernel(res_n, seq_n, *refs):
    count = len(ARGS)
    loads = Loads(refs[:count], refs[count + 2 : 2 * count + 2], refs[2 * count + 2])
    msa_out, pair_out = refs[count : count + 2]
    (
        rows_all,
        in_send,
        in_all,
        up_send,
        up_all,
        back_send,
        back_all,
        right_all,
        right_f32,
        left_all,
        msa_res,
        pair_res,
        key_buf,
        val_buf,
        t_buf,
        rows_ss,
        rows_rs,
        in_ss,
        in_rs,
        up_ss,
        up_rs,
        back_ss,
        back_rs,
        rz_ss,
        rz_rs,
        rr_ss,
        rr_rs,
        left_ss,
        left_rs,
        out_sems,
    ) = refs[2 * count + 3 :]
    loads.start(LOAD_ORDER[:2])
    me_r = lax.axis_index("res")
    me_z = lax.axis_index("seq")
    s_loc, i_loc, width = loads.places["msa"].shape
    residues = loads.places["pair"].shape[1]
    rows = s_loc * i_loc
    share = i_loc // seq_n
    seqs = s_loc * seq_n
    block = share * s_loc
    scale = HEAD_DIM ** (-0.5)

    chips = res_n // 2
    core = lax.rem(me_r, 2)
    sibling = me_r + 1 - 2 * core

    def chip_peer(d):
        return lax.rem(me_r + 2 * d, res_n)

    class ResGather:
        def __init__(self, buffer, ss, rs):
            self.buffer, self.ss, self.rs = buffer, ss, rs
            self.direct = {}
            self.passed = {}

        def copy(self, at, slot, peer):
            return send_res(self.buffer.at[at], self.ss.at[slot], self.rs.at[slot], peer)

        def start(self):
            for d in range(1, chips):
                self.direct[d] = self.copy(me_r, d, chip_peer(d))
                self.direct[d].start()
            self.passed[0] = self.copy(me_r, chips, sibling)
            self.passed[0].start()

        def arrive(self, d):
            self.direct[d].wait_recv()
            src = lax.rem(me_r - 2 * d + res_n, res_n)
            self.passed[d] = self.copy(src, chips + d, sibling)
            self.passed[d].start()
            return src

        def arrive_passed(self, d):
            self.passed[d].wait_recv()
            return lax.rem(sibling - 2 * d + res_n, res_n)

        def finish(self):
            for c in list(self.direct.values()) + list(self.passed.values()):
                c.wait_send()

    def seq_peer(d):
        return lax.rem(me_z + d, seq_n)

    def send_res(ref, ss, rs, peer):
        return pltpu.make_async_remote_copy(
            src_ref=ref, dst_ref=ref, send_sem=ss, recv_sem=rs,
            device_id=(peer, me_z), device_id_type=MESH,
        )

    def send_seq(src, dst, ss, rs, d):
        return pltpu.make_async_remote_copy(
            src_ref=src, dst_ref=dst, send_sem=ss, recv_sem=rs,
            device_id=(me_r, seq_peer(d)), device_id_type=MESH,
        )

    barrier = pltpu.get_barrier_semaphore()
    for peer in [chip_peer(d) for d in range(1, chips)] + [sibling]:
        pl.semaphore_signal(barrier, inc=1, device_id=(peer, me_z), device_id_type=MESH)
    for d in range(1, seq_n):
        pl.semaphore_signal(barrier, inc=1, device_id=(me_r, seq_peer(d)), device_id_type=MESH)

    loads.start(LOAD_ORDER[2:])
    msa = loads["msa"][...].astype(F32).reshape(rows, width)
    normed = normalize_layer(msa, row(loads["row_gain"])).astype(BF16)
    rows_all[me_r] = normed
    to_cols = swap_matrix(s_loc, i_loc)
    in_send[...] = mm(to_cols, msa.astype(BF16)).astype(BF16)

    pl.semaphore_wait(barrier, chips + seq_n - 1)
    row_gather = ResGather(rows_all, rows_ss, rows_rs)
    row_gather.start()
    in_sends = []
    for d in range(1, seq_n):
        start = pl.multiple_of(seq_peer(d) * block, block)
        c = send_seq(in_send.at[pl.ds(start, block)], in_all.at[me_z], in_ss.at[d], in_rs.at[d], d)
        c.start()
        in_sends.append(c)
    own = pl.multiple_of(me_z * block, block)
    in_all[me_z] = in_send[pl.ds(own, block)]

    pair_f32 = loads["pair"][...].astype(F32).reshape(i_loc * residues, PAIR_CH)
    pair_normed = normalize_layer(pair_f32, row(loads["pair_gain"])).astype(BF16)
    bias_t = loads["bias_w"][...]
    by_residue = [
        mm_nt(bias_t, pair_normed[i * residues : (i + 1) * residues]) for i in range(i_loc)
    ]
    by_residue = jnp.concatenate(by_residue, axis=0).astype(BF16)
    bias = mm(swap_matrix(i_loc, HEADS), by_residue)

    mask = head_mask(width)
    queries = mm(normed, loads["rq"][...])
    gate = jax.nn.sigmoid(mm(normed, loads["rg"][...]) + row(loads["rgb"]))

    def keys_of(src, data):
        key_buf[src] = mm(data, loads["rk"][...]).reshape(s_loc, i_loc, width)
        val_buf[src] = mm(data, loads["rv"][...]).reshape(s_loc, i_loc, width)

    keys_of(me_r, normed)
    half = FACTOR_WIDTH // 2
    spread = [
        jnp.concatenate(
            [
                loads["ow"][pl.ds(e, FACTOR_WIDTH, stride=FACTOR_WIDTH), :]
                for e in (k, half + k)
            ],
            axis=1,
        ).astype(BF16)
        for k in range(half)
    ]
    src = row_gather.arrive_passed(0)
    keys_of(src, rows_all[src])
    for d in range(1, chips):
        src = row_gather.arrive(d)
        keys_of(src, rows_all[src])
    for d in range(1, chips):
        src = row_gather.arrive_passed(d)
        keys_of(src, rows_all[src])

    scores = []
    for s in range(s_loc):
        q = queries[s * i_loc : (s + 1) * i_loc]
        q = (q[None] * mask).reshape(HEADS * i_loc, width).astype(BF16)
        k = key_buf[:, s].reshape(residues, width).astype(BF16)
        scores.append(mm_nt(q, k) * scale + bias)
    probs = [softmax_rows(x) for x in scores]
    attended = []
    for s in range(s_loc):
        v = val_buf[:, s].reshape(residues, width).astype(BF16)
        o = mm(probs[s], v).reshape(HEADS, i_loc, width)
        attended.append(jnp.sum(o * mask, axis=0))
    attended = jnp.concatenate(attended, axis=0)
    update = (mm((gate * attended).astype(BF16), loads["ro"][...]) + row(loads["rob"])).astype(BF16)
    up_send[...] = mm(to_cols, update).astype(BF16)
    up_sends = []
    for d in range(1, seq_n):
        start = pl.multiple_of(seq_peer(d) * block, block)
        c = send_seq(up_send.at[pl.ds(start, block)], up_all.at[me_z], up_ss.at[d], up_rs.at[d], d)
        c.start()
        up_sends.append(c)
    up_all[me_z] = up_send[pl.ds(own, block)]
    for c in in_sends:
        c.wait_recv()
    for c in up_sends:
        c.wait_recv()

    both = in_all[...].astype(F32) + up_all[...].astype(F32)
    both = both.reshape(seq_n, share, s_loc, width)
    first = jnp.concatenate([both[:, a].reshape(seqs, width) for a in range(share)], axis=0)
    normed = normalize_layer(first, row(loads["col_gain"])).astype(BF16)
    queries = mm(normed, loads["cq"][...])
    keys = mm(normed, loads["ck"][...]).astype(BF16)
    values = mm(normed, loads["cv"][...]).astype(BF16)
    gate = jax.nn.sigmoid(mm(normed, loads["cg"][...]) + row(loads["cgb"]))
    attended = []
    for a in range(share):
        at = slice(a * seqs, (a + 1) * seqs)
        q = (queries[at][None] * mask).reshape(HEADS * seqs, width).astype(BF16)
        p = softmax_rows(mm_nt(q, keys[at]) * scale)
        o = mm(p, values[at]).reshape(HEADS, seqs, width)
        attended.append(jnp.sum(o * mask, axis=0))
    attended = jnp.concatenate(attended, axis=0)
    update = (mm((gate * attended).astype(BF16), loads["co"][...]) + row(loads["cob"])).astype(BF16)
    second = first + update.astype(F32)
    normed = normalize_layer(second, row(loads["tr_gain"])).astype(BF16)
    hidden = jnp.maximum(mm(normed, loads["ti"][...]) + row(loads["tib"]), 0.0).astype(BF16)
    final = (second + mm(hidden, loads["to"][...]) + row(loads["tob"])).astype(BF16)

    normed = normalize_layer(final.astype(F32), row(loads["op_gain"])).astype(BF16)
    right = mm_nt(loads["wr"][...], normed)
    right = jnp.concatenate(
        [
            jnp.concatenate(
                [right[:half, a * seqs : (a + 1) * seqs], right[half:, a * seqs : (a + 1) * seqs]],
                axis=1,
            )
            for a in range(share)
        ],
        axis=0,
    )
    right_all[me_r, me_z] = right.astype(BF16)
    here = right_all.at[me_r, me_z]
    rz_sends = []
    for d in range(1, seq_n):
        c = send_seq(here, here, rz_ss.at[d], rz_rs.at[d], d)
        c.start()
        rz_sends.append(c)
    left_all[me_z] = mm_nt(loads["wl"][...], normed).astype(BF16)
    here = left_all.at[me_z]
    left_sends = []
    for d in range(1, seq_n):
        c = send_seq(here, here, left_ss.at[d], left_rs.at[d], d)
        c.start()
        left_sends.append(c)

    for t in range(seq_n):
        back_send[t] = jnp.concatenate(
            [final[a * seqs + t * s_loc : a * seqs + (t + 1) * s_loc] for a in range(share)],
            axis=0,
        )
    back_sends = []
    for d in range(1, seq_n):
        c = send_seq(
            back_send.at[seq_peer(d)], back_all.at[me_z], back_ss.at[d], back_rs.at[d], d
        )
        c.start()
        back_sends.append(c)
    back_all[me_z] = back_send[me_z]

    for c in rz_sends:
        c.wait_recv()
    right_gather = ResGather(right_all, rr_ss, rr_rs)
    right_gather.start()

    def left_term(t):
        left = left_all[t].astype(F32).T.astype(BF16)
        for k in range(half):
            term = mm(left, spread[k])
            for p in range(2):
                t_buf[t, pl.ds((2 * k + p) * seqs, seqs), :] = jnp.concatenate(
                    [
                        term[a * seqs : (a + 1) * seqs, p * PAIR_CH : (p + 1) * PAIR_CH]
                        for a in range(share)
                    ],
                    axis=1,
                ).astype(BF16)

    left_term(me_z)
    for k in range(1, seq_n):
        left_sends[k - 1].wait_recv()
        left_term(lax.rem(me_z - k + seq_n, seq_n))
        if k == 1:
            for d in range(1, chips):
                right_gather.arrive(d)

    for c in back_sends:
        c.wait_recv()
    from_cols = swap_matrix(i_loc, s_loc)
    back = mm(from_cols, back_all[...].reshape(rows, width))
    msa_res[...] = back.reshape(s_loc, i_loc, width).astype(BF16)
    msa_copy = pltpu.make_async_copy(msa_res, msa_out, out_sems.at[0])
    msa_copy.start()

    for d in range(chips):
        right_gather.arrive_passed(d)
    right_f32[...] = right_all[...].astype(F32).reshape(right_f32.shape)
    right_rows = jnp.concatenate(
        [right_f32[pl.ds(k, residues, stride=half), :].astype(BF16) for k in range(half)], axis=1
    )
    bias_out = row(loads["ob"])
    for t in range(seq_n):
        change = mm(right_rows, t_buf[t]) * (1.0 / seqs)
        for a in range(share):
            old = loads["pair"][t * share + a].astype(F32)
            new = old + change[:, a * PAIR_CH : (a + 1) * PAIR_CH] + bias_out
            pair_res[t * share + a] = new.astype(BF16)
    pair_copy = pltpu.make_async_copy(pair_res, pair_out, out_sems.at[1])
    pair_copy.start()
    for c in in_sends + up_sends + rz_sends + left_sends + back_sends:
        c.wait_send()
    row_gather.finish()
    right_gather.finish()
    msa_copy.wait()
    pair_copy.wait()


def copy_kernel(msa_in, pair_in, msa_out, pair_out, msa_held, pair_held, sems):
    loads = [
        pltpu.make_async_copy(msa_in, msa_held, sems.at[0]),
        pltpu.make_async_copy(pair_in, pair_held, sems.at[1]),
    ]
    stores = [
        pltpu.make_async_copy(msa_held, msa_out, sems.at[2]),
        pltpu.make_async_copy(pair_held, pair_out, sems.at[3]),
    ]
    for c in loads:
        c.start()
    for c, after in zip(loads, stores):
        c.wait()
        after.start()
    for c in stores:
        c.wait()


def kernel_body(res_n, seq_n, *args):
    args = [a.T if name in ("bias_w", "wl", "wr") else a for name, a in zip(ARGS, args)]
    msa, pair = args[:2]
    s_loc, i_loc, width = msa.shape
    residues = pair.shape[1]
    rows = s_loc * i_loc
    share = i_loc // seq_n
    seqs = s_loc * seq_n
    block = share * s_loc
    factor_rows = share * FACTOR_WIDTH // 2
    dma = pltpu.SemaphoreType.DMA
    scratch = [pltpu.VMEM(a.shape, a.dtype) for a in args] + [dma((len(args),))]
    scratch += [
        pltpu.VMEM((res_n, rows, width), BF16),
        pltpu.VMEM((rows, width), BF16),
        pltpu.VMEM((seq_n, block, width), BF16),
        pltpu.VMEM((rows, width), BF16),
        pltpu.VMEM((seq_n, block, width), BF16),
        pltpu.VMEM((seq_n, block, width), BF16),
        pltpu.VMEM((seq_n, block, width), BF16),
        pltpu.VMEM((res_n, seq_n, factor_rows, 2 * seqs), BF16),
        pltpu.VMEM((res_n * seq_n * factor_rows, 2 * seqs), F32),
        pltpu.VMEM((seq_n, FACTOR_WIDTH, rows), BF16),
        pltpu.VMEM(msa.shape, BF16),
        pltpu.VMEM(pair.shape, BF16),
        pltpu.VMEM((res_n, s_loc, i_loc, width), F32),
        pltpu.VMEM((res_n, s_loc, i_loc, width), F32),
        pltpu.VMEM((seq_n, FACTOR_WIDTH * seqs, share * PAIR_CH), BF16),
    ]
    scratch += [dma((res_n,))] * 2 + [dma((seq_n,))] * 8
    scratch += [dma((res_n,))] * 2 + [dma((seq_n,))] * 2 + [dma((2,))]
    hbm = pl.BlockSpec(memory_space=pltpu.HBM)
    shapes = (
        jax.ShapeDtypeStruct(msa.shape, BF16),
        jax.ShapeDtypeStruct(pair.shape, BF16),
    )
    results = pl.pallas_call(
        functools.partial(block_kernel, res_n, seq_n),
        out_shape=shapes,
        in_specs=[hbm] * len(args),
        out_specs=(hbm, hbm),
        scratch_shapes=scratch,
        compiler_params=pltpu.CompilerParams(
            collective_id=0, has_side_effects=True, vmem_limit_bytes=64 * 1024 * 1024
        ),
        name="msa_block",
    )(*args)
    return pl.pallas_call(
        copy_kernel,
        out_shape=shapes,
        in_specs=[hbm] * 2,
        out_specs=(hbm, hbm),
        scratch_shapes=[pltpu.VMEM(msa.shape, BF16), pltpu.VMEM(pair.shape, BF16), dma((4,))],
        compiler_params=pltpu.CompilerParams(vmem_limit_bytes=64 * 1024 * 1024),
        name="results",
    )(*results)


def body(*args):
    msa = args[0]
    res_n = lax.axis_size("res")
    seq_n = lax.axis_size("seq")
    share = msa.shape[1] // seq_n
    small = (
        msa.shape[0] == 16
        and msa.shape[1] == 8
        and share == 2
        and msa.shape[0] * seq_n == 64
        and res_n * msa.shape[1] == 64
    )
    if small:
        return kernel_body(res_n, seq_n, *args)
    return spread_body(*args)


def solution(mesh):
    return jax.shard_map(
        body,
        mesh=mesh,
        in_specs=(
            P("seq", "res", None),
            P("res", None, None),
            P(),
            P(),
            P(),
            P(),
            P(),
            P(),
            P(),
            P(),
            P(),
            P(),
            P(),
            P(),
            P(),
            P(),
            P(),
            P(),
            P(),
            P(),
            P(),
            P(),
            P(),
            P(),
            P(),
            P(),
            P(),
            P(),
            P(),
            P(),
        ),
        out_specs=(P("seq", "res", None), P("res", None, None)),
        check_vma=False,
    )
```
